128 devices in a mesh: row: 8 (over x, core), col: 16 (over y, z).
Axes of the slice: x: 4, y: 4, z: 4, core: 2. Of those that a mesh axis runs over, the one named last changes fastest.
Arguments:
- left_h: float32 [16384, 512], P('row', 'col'), may hold values from 0 to 3.0517578e-05
- left_l: float32 [16384, 512], P('row', 'col'), may hold values from 0 to 3.0517578e-05
- right_h: float32 [512, 16384], P('row', 'col'), may hold values from 0 to 3.0517578e-05
- right_l: float32 [512, 16384], P('row', 'col'), may hold values from 0 to 3.0517578e-05
Outputs:
- cross_sum: float32 [16384, 16384], P('row', 'col')
- square_h: float32 [16384, 16384], P('row', 'col')
- square_l: float32 [16384, 16384], P('row', 'col')
The draws below stay inside these ranges and needn't reach their ends.
All inputs are finite; a program needn't handle non-finite values.
Results may differ from the reference program's by a relative error of at most 0.00005.
Values sent between devices are 32-bit elements; how exact they have to be, the bound alone decides.
A program may use at most 128 MiB of HBM per device.

```python
import jax
import jax.numpy as jnp
from jax import lax

ORDER = 16384
KW = 512
ROWS = 16384


def block_scale(own_key, dims, pieces, least, largest):
    gain, own = 1.0, jax.random.fold_in(own_key, 6)
    for axis_at, shards_of in pieces:
        draws = jnp.exp(jax.random.uniform(jax.random.fold_in(own, axis_at), (shards_of,), jnp.float32, least / len(pieces), largest / len(pieces)))
        gain = gain * jnp.repeat(draws, dims[axis_at] // shards_of).reshape([-1 if axis == axis_at else 1 for axis in range(len(dims))])
    return gain


def setup_inputs(seed: int = 0) -> dict:
    seeds = jax.random.split(jax.random.key(seed), 5)
    return {
        "left_h": jnp.clip(3.0517578125e-05 * jax.random.uniform(seeds[0], (ROWS, KW), jnp.float32) ** block_scale(seeds[0], (ROWS, KW), ((0, 8), (1, 16)), -0.2, 0.2), 0.0, 3.0517578125e-05),
        "left_l": jnp.clip(3.0517578125e-05 * jax.random.uniform(seeds[1], (ROWS, KW), jnp.float32) ** block_scale(seeds[1], (ROWS, KW), ((0, 8), (1, 16)), -0.2, 0.2), 0.0, 3.0517578125e-05),
        "right_h": jnp.clip(3.0517578125e-05 * jax.random.uniform(seeds[2], (KW, ORDER), jnp.float32) ** block_scale(seeds[2], (KW, ORDER), ((0, 8), (1, 16)), -0.2, 0.2), 0.0, 3.0517578125e-05),
        "right_l": jnp.clip(3.0517578125e-05 * jax.random.uniform(seeds[3], (KW, ORDER), jnp.float32) ** block_scale(seeds[3], (KW, ORDER), ((0, 8), (1, 16)), -0.2, 0.2), 0.0, 3.0517578125e-05),
    }


def product(left, right):
    return jnp.dot(left, right, preferred_element_type=jnp.float32, precision=lax.Precision.HIGHEST)


def reference(left_h, left_l, right_h, right_l):
    factor = (2.0 ** 30) / KW
    square_h = factor * product(left_h, right_h)
    square_l = factor * product(left_l, right_l)
    cross_sum = factor * (product(left_h, right_l) + product(left_l, right_h))
    return cross_sum, square_h, square_l
```

```python
import functools

import jax
import jax.numpy as jnp
from jax import lax
from jax.experimental import pallas as pl
from jax.experimental.pallas import tpu as pltpu
from jax.sharding import PartitionSpec as P

KW = 512
SCALE = 2.0**30 / KW
MESH = pl.DeviceIdType.MESH
F32, BF16 = jnp.float32, jnp.bfloat16

M, N, KD, RD = 2048, 1024, 32, 64
CH = 512
NCH = M // CH
EARLY = NCH - 1
SUB = CH // 4

dot = functools.partial(jnp.dot, preferred_element_type=F32)


def split(value):
    high = value.astype(BF16)
    return high, (value - high.astype(F32)).astype(BF16)


def times_hh(a, b, rows):
    return SCALE * (dot(a[rows, 0:1024], b[1024:2048, :]) + dot(a[rows, 512:1024], b[1024:1536, :]))


def times_ll(a, b, rows):
    return SCALE * (dot(a[rows, 1024:2048], b[0:1024, :]) + dot(a[rows, 1536:2048], b[0:512, :]))


def times_cross(a, b, rows):
    small = dot(a[rows, :], b[:, :])
    return SCALE * (small + (dot(a[rows, 512:1024], b[0:512, :]) + dot(a[rows, 1536:2048], b[1024:1536, :])))


def gather_kernel(
    lth, ltl, rth, rtl,
    out_c, out_h, out_l, a_last, b,
    lt, rl, rr, a, load_sem,
    s1s, s1r, s2s, s2r, s3s, s3r, s4s, s4r, rs, rv,
):
    row, col = lax.axis_index("row"), lax.axis_index("col")
    x, core, y, z = row // 2, row % 2, col // 4, col % 4

    def wrap(v):
        return lax.rem(v + 8, 4)

    def at(dx=0, dc=0, dy=0, dz=0):
        new_core = 1 - core if dc else core
        return (wrap(x + dx) * 2 + new_core, wrap(y + dy) * 4 + wrap(z + dz))

    step = (1, -1)
    yz = tuple(tuple(at(dy=d) if ax == 0 else at(dz=d) for d in step) for ax in (0, 1))
    xs = tuple(at(dx=d) for d in step)
    twin = at(dc=1)

    loads = [pltpu.make_async_copy(ref, lt.at[i], load_sem.at[i]) for i, ref in enumerate((lth, ltl))]
    own_right = [pltpu.make_async_copy(ref, rr.at[i, row], load_sem.at[2 + i]) for i, ref in enumerate((rth, rtl))]
    for copy in loads + own_right:
        copy.start()
    barrier = pltpu.get_barrier_semaphore()
    for device in (*yz[0], *yz[1], *xs, twin):
        pl.semaphore_signal(barrier, 1, device_id=device, device_id_type=MESH)
    for copy in loads:
        copy.wait()

    for c in range(NCH):
        for arr in (0, 1):
            parts = []
            for p in range(4):
                start = pl.multiple_of(c * CH + wrap(p - z) * SUB, SUB)
                parts.append(lt[arr, :, pl.ds(start, SUB)])
            rl[arr, y, z, c] = jnp.concatenate(parts, axis=0).T

    pl.semaphore_wait(barrier, 7)
    started = []

    def send(src, dst, send_sem, recv_sem, device):
        copy = pltpu.make_async_remote_copy(
            src_ref=src, dst_ref=dst, send_sem=send_sem, recv_sem=recv_sem, device_id=device, device_id_type=MESH
        )
        copy.start()
        started.append(copy)

    def arrived(ref, sem):
        pltpu.make_async_copy(ref, ref, sem).wait()

    off = (0, -1, 1, 2)
    opp = (1, 0)

    def tile(arr, first, second, c):
        f, s = wrap((y, z)[arr] + first), wrap((z, y)[arr] + second)
        return rl.at[arr, f, s, c] if arr == 0 else rl.at[arr, s, f, c]

    def line(arr, second, c):
        s = wrap((z, y)[arr] + second)
        return rl.at[arr, :, s, c] if arr == 0 else rl.at[arr, s, :, c]

    def half(ref, d):
        rows = pl.ds(d * (SUB // 2), SUB // 2)
        return ref.at[rows] if len(ref.shape) == 2 else ref.at[:, rows]

    def s1_send(c):
        for d in (0, 1):
            for arr in (0, 1):
                ref = tile(arr, 0, 0, c)
                send(ref, ref, s1s.at[c, arr, d], s1r.at[c, arr, d], yz[arr][d])

    def s1_wait(c, d):
        for arr in (0, 1):
            arrived(tile(arr, -step[d], 0, c), s1r.at[c, arr, d])

    def s2_send(c, d):
        for arr in (0, 1):
            ref = half(tile(arr, -step[d], 0, c), d)
            send(ref, ref, s2s.at[c, arr, d], s2r.at[c, arr, d], yz[arr][d])

    def s2_wait(c):
        for arr in (0, 1):
            for d in (0, 1):
                arrived(half(tile(arr, 2, 0, c), d), s2r.at[c, arr, d])

    def s3_send(c, k):
        for d in (0, 1):
            for arr in (0, 1):
                ref = tile(arr, off[k], 0, c)
                send(ref, ref, s3s.at[c, arr, d, k], s3r.at[c, arr, d, k], yz[1 - arr][d])

    def s3_wait(c, k, d):
        for arr in (0, 1):
            arrived(tile(arr, off[k], -step[d], c), s3r.at[c, arr, d, k])

    def s4_send(c, k, d):
        for arr in (0, 1):
            ref = half(tile(arr, off[k], -step[d], c), d)
            send(ref, ref, s4s.at[c, arr, d, k], s4r.at[c, arr, d, k], yz[1 - arr][d])

    def s4_wait(c, k):
        for arr in (0, 1):
            for d in (0, 1):
                arrived(half(tile(arr, off[k], 2, c), d), s4r.at[c, arr, d, k])

    def s3_line_send(c):
        for d in (0, 1):
            for arr in (0, 1):
                ref = line(arr, 0, c)
                send(ref, ref, s3s.at[c, arr, d, 0], s3r.at[c, arr, d, 0], yz[1 - arr][d])

    def s4_line_send(c, lines):
        for d in (0, 1):
            for arr in (0, 1):
                if lines:
                    arrived(line(arr, -step[d], c), s3r.at[c, arr, d, 0])
                else:
                    for k in range(4):
                        arrived(tile(arr, off[k], -step[d], c), s3r.at[c, arr, d, k])
                ref = half(line(arr, -step[d], c), d)
                send(ref, ref, s4s.at[c, arr, d, 0], s4r.at[c, arr, d, 0], yz[1 - arr][d])

    def s4_line_wait(c):
        for arr in (0, 1):
            for d in (0, 1):
                arrived(half(line(arr, 2, c), d), s4r.at[c, arr, d, 0])

    def shard(dx, other=False):
        return wrap(x + dx) * 2 + (1 - core if other else core)

    def right_first():
        for d in (0, 1):
            for arr in (0, 1):
                send((rth, rtl)[arr], rr.at[arr, row], rs.at[0, arr, d], rv.at[0, arr, d], xs[d])
        for arr in (0, 1):
            send((rth, rtl)[arr], rr.at[arr, row], rs.at[1, arr, 0], rv.at[1, arr, 0], twin)

    def right_second(d):
        for arr in (0, 1):
            arrived(rr.at[arr, shard(-step[d])], rv.at[0, arr, d])
        ref = rr.at[d, shard(-step[d])]
        send(ref, ref, rs.at[2, d, 0], rv.at[2, d, 0], xs[d])
        for arr in (0, 1):
            ref = rr.at[arr, shard(-step[d])]
            send(ref, ref, rs.at[3 + d, arr, 0], rv.at[3 + d, arr, 0], twin)

    def right_third():
        for d in (0, 1):
            ref = rr.at[d, shard(2)]
            arrived(ref, rv.at[2, d, 0])
            send(ref, ref, rs.at[5, d, 0], rv.at[5, d, 0], twin)

    def split_right(index):
        rows = pl.multiple_of(index * RD, RD)
        for arr, base in ((0, 1024), (1, 0)):
            high, low = split(rr[arr, index])
            b[pl.ds(base + rows, RD), :] = high
            b[pl.ds(base + 512 + rows, RD), :] = low

    s1_send(0)
    right_first()
    s3_send(0, 0)
    for c in (1, 2, 3):
        s1_send(c)
    for copy in own_right:
        copy.wait()
    split_right(row)
    for d in (0, 1):
        s1_wait(0, d)
        s2_send(0, d)
    for k in (1, 2):
        s3_send(0, k)
    s2_wait(0)
    s3_send(0, 3)
    for c in (1, 2, 3):
        for d in (0, 1):
            s1_wait(c, d)
            s2_send(c, d)
    s3_send(1, 0)
    for arr in (0, 1):
        arrived(rr.at[arr, shard(0, True)], rv.at[1, arr, 0])
    split_right(shard(0, True))
    for d in (0, 1):
        right_second(d)
    for d in (0, 1):
        s3_wait(0, 0, d)
        s4_send(0, 0, d)
    for k in (1, 2):
        s3_send(1, k)
    for k in (1, 2):
        for d in (0, 1):
            s3_wait(0, k, d)
            s4_send(0, k, d)
    s2_wait(1)
    for d in (0, 1):
        s3_wait(0, 3, d)
        s4_send(0, 3, d)
    s3_send(1, 3)
    for d in (0, 1):
        split_right(shard(-step[d]))
    for d in (0, 1):
        for arr in (0, 1):
            arrived(rr.at[arr, shard(-step[d], True)], rv.at[3 + d, arr, 0])
        split_right(shard(-step[d], True))
    right_third()
    split_right(shard(2))
    for arr in (0, 1):
        arrived(rr.at[arr, shard(2, True)], rv.at[5, arr, 0])
    split_right(shard(2, True))
    s2_wait(2)
    s2_wait(3)

    lane = lax.broadcasted_iota(jnp.int32, (SUB, 128), 1) // KD

    def collect(c, target):
        def body(g, carry):
            for arr in (0, 1):
                for j in range(4):
                    value = rl[arr, g, (3 - j) % 4, c]
                    for p in range(3):
                        value = jnp.where(lane == p, rl[arr, g, (p - j) % 4, c], value)
                    if j:
                        value = pltpu.roll(value, 128 - KD * j, 1)
                    high, low = split(value)
                    cols = pl.multiple_of(arr * 1024 + g * 128, 128)
                    target[pl.ds(j * SUB, SUB), pl.ds(cols, 128)] = low
                    target[pl.ds(j * SUB, SUB), pl.ds(cols + 512, 128)] = high
            return carry

        lax.fori_loop(0, 4, body, 0)

    def multiply(c, u):
        src = pl.ds(u * 256, 256)
        dst = pl.ds(c * CH + u * 256, 256)
        out_h[dst, :] = times_hh(a, b, src)
        out_l[dst, :] = times_ll(a, b, src)
        out_c[dst, :] = times_cross(a, b, src)

    for c in range(EARLY):
        if c == 0:
            for k in range(4):
                s4_wait(0, k)
        else:
            s4_line_wait(c)
        if c + 2 < NCH:
            s3_line_send(c + 2)
        collect(c, a)
        multiply(c, 0)
        s4_line_send(c + 1, c + 1 >= 2)
        multiply(c, 1)
    s4_line_wait(EARLY)
    collect(EARLY, a_last)
    for copy in started:
        copy.wait_send()


def finish_kernel(c_in, h_in, l_in, a, b, c_out, h_out, l_out, stage, early_sem, late_sem):
    copies = []
    for i, (src, dst) in enumerate(((c_in, c_out), (h_in, h_out), (l_in, l_out))):
        for q in range(EARLY):
            rows = pl.ds(q * CH, CH)
            copies.append(pltpu.make_async_copy(src.at[rows], dst.at[rows], early_sem.at[i, q]))
            copies[-1].start()
    for u in range(2):
        rows = pl.ds(u * 256, 256)
        for i, (times, dst) in enumerate(((times_cross, c_out), (times_hh, h_out), (times_ll, l_out))):
            stage[i, rows] = times(a, b, rows)
            copies.append(
                pltpu.make_async_copy(
                    stage.at[i, rows], dst.at[pl.ds(EARLY * CH + u * 256, 256)], late_sem.at[i, u]
                )
            )
            copies[-1].start()
    for copy in copies:
        copy.wait()


def per_device(left_h, left_l, right_h, right_l):
    dma = pltpu.SemaphoreType.DMA
    hbm, vmem = pl.BlockSpec(memory_space=pl.ANY), pl.BlockSpec(memory_space=pltpu.VMEM)
    early = pl.pallas_call(
        gather_kernel,
        out_shape=[pltpu.VMEM((EARLY * CH, N), F32)] * 3
        + [pltpu.VMEM((CH, 4 * KW), BF16), pltpu.VMEM((4 * KW, N), BF16)],
        in_specs=[hbm] * 4,
        out_specs=[vmem] * 5,
        scratch_shapes=[
            pltpu.VMEM((2, KD, M), F32),
            pltpu.VMEM((2, 4, 4, NCH, SUB, 128), F32),
            pltpu.VMEM((2, 8, RD, N), F32),
            pltpu.VMEM((CH, 4 * KW), BF16),
            dma((4,)),
            dma((NCH, 2, 2)), dma((NCH, 2, 2)), dma((NCH, 2, 2)), dma((NCH, 2, 2)),
            dma((NCH, 2, 2, 4)), dma((NCH, 2, 2, 4)), dma((NCH, 2, 2, 4)), dma((NCH, 2, 2, 4)),
            dma((6, 2, 2)), dma((6, 2, 2)),
        ],
        compiler_params=pltpu.CompilerParams(
            collective_id=0, has_side_effects=True, vmem_limit_bytes=22 << 20
        ),
        cost_estimate=pl.CostEstimate(flops=18 * M * N * KW, bytes_accessed=2 << 20, transcendentals=0),
        name="gather_multiply",
    )(left_h.T, left_l.T, right_h, right_l)
    return pl.pallas_call(
        finish_kernel,
        out_shape=[jax.ShapeDtypeStruct((M, N), F32)] * 3,
        in_specs=[vmem] * 5,
        out_specs=[hbm] * 3,
        scratch_shapes=[pltpu.VMEM((3, CH, N), F32), dma((3, EARLY)), dma((3, 2))],
        compiler_params=pltpu.CompilerParams(vmem_limit_bytes=10 << 20),
        cost_estimate=pl.CostEstimate(flops=6 * M * N * KW, bytes_accessed=24 << 20, transcendentals=0),
        name="multiply_write",
    )(*(pltpu.with_memory_space_constraint(v, pltpu.VMEM) for v in early))


def solution(mesh):
    spec = P("row", "col")
    return jax.shard_map(
        per_device, mesh=mesh, in_specs=(spec,) * 4, out_specs=(spec,) * 3, check_vma=False
    )
```

```python
import functools

import jax
import jax.numpy as jnp
from jax import lax
from jax.experimental import pallas as pl
from jax.experimental.pallas import tpu as pltpu
from jax.sharding import PartitionSpec as P

KW = 512
SCALE = 2.0**30 / KW
MESH = pl.DeviceIdType.MESH
F32, BF16 = jnp.float32, jnp.bfloat16

M, N, KD, RD = 2048, 1024, 32, 64
CH = 512
NCH = M // CH
EARLY = NCH - 1
SUB = CH // 4

dot = functools.partial(jnp.dot, preferred_element_type=F32)


def split(value):
    high = value.astype(BF16)
    return high, (value - high.astype(F32)).astype(BF16)


def times_hh(a, b, rows):
    return SCALE * (dot(a[rows, 0:1024], b[1024:2048, :]) + dot(a[rows, 512:1024], b[1024:1536, :]))


def times_ll(a, b, rows):
    return SCALE * (dot(a[rows, 1024:2048], b[0:1024, :]) + dot(a[rows, 1536:2048], b[0:512, :]))


def times_cross(a, b, rows):
    small = dot(a[rows, :], b[:, :])
    return SCALE * (small + (dot(a[rows, 512:1024], b[0:512, :]) + dot(a[rows, 1536:2048], b[1024:1536, :])))


def gather_kernel(
    lth, ltl, rth, rtl,
    out_c, out_h, out_l, a_last, b,
    lt, rl, rr, a, load_sem,
    near_sent, far_sent, right_sent, s1r, s2r, s3r, s4r, rv,
):
    row, col = lax.axis_index("row"), lax.axis_index("col")
    x, core, y, z = row // 2, row % 2, col // 4, col % 4

    def wrap(v):
        return lax.rem(v + 8, 4)

    def at(dx=0, dc=0, dy=0, dz=0):
        new_core = 1 - core if dc else core
        return (wrap(x + dx) * 2 + new_core, wrap(y + dy) * 4 + wrap(z + dz))

    step = (1, -1)
    yz = tuple(tuple(at(dy=d) if ax == 0 else at(dz=d) for d in step) for ax in (0, 1))
    xs = tuple(at(dx=d) for d in step)
    twin = at(dc=1)

    loads = [pltpu.make_async_copy(ref, lt.at[i], load_sem.at[i]) for i, ref in enumerate((lth, ltl))]
    own_right = [pltpu.make_async_copy(ref, rr.at[i, row], load_sem.at[2 + i]) for i, ref in enumerate((rth, rtl))]
    for copy in loads + own_right:
        copy.start()
    barrier = pltpu.get_barrier_semaphore()
    for device in (*yz[0], *yz[1], *xs, twin):
        pl.semaphore_signal(barrier, 1, device_id=device, device_id_type=MESH)
    for copy in loads:
        copy.wait()

    def pack(c):
        for arr in (0, 1):
            parts = []
            for p in range(4):
                start = pl.multiple_of(c * CH + wrap(p - z) * SUB, SUB)
                parts.append(lt[arr, :, pl.ds(start, SUB)])
            rl[arr, y, z, c] = jnp.concatenate(parts, axis=0).T

    pack(0)
    pl.semaphore_wait(barrier, 7)

    def send(src, dst, send_sem, recv_sem, device):
        pltpu.make_async_remote_copy(
            src_ref=src, dst_ref=dst, send_sem=send_sem, recv_sem=recv_sem, device_id=device, device_id_type=MESH
        ).start()

    def arrived(ref, sem):
        pltpu.make_async_copy(ref, ref, sem).wait()

    off = (0, -1, 1, 2)
    both = [(d, arr) for d in (0, 1) for arr in (0, 1)]

    def tile(arr, first, second, c):
        f, s = wrap((y, z)[arr] + first), wrap((z, y)[arr] + second)
        return rl.at[arr, f, s, c] if arr == 0 else rl.at[arr, s, f, c]

    def line(arr, second, c):
        s = wrap((z, y)[arr] + second)
        return rl.at[arr, :, s, c] if arr == 0 else rl.at[arr, s, :, c]

    def half(ref, d):
        rows = pl.ds(d * (SUB // 2), SUB // 2)
        return ref.at[rows] if len(ref.shape) == 2 else ref.at[:, rows]

    def s1_send(c):
        for d, arr in both:
            ref = tile(arr, 0, 0, c)
            send(ref, ref, near_sent.at[0], s1r.at[c], yz[arr][d])

    def s2_send(c):
        arrived(rl.at[0, 0, :, c], s1r.at[c])
        for d, arr in both:
            ref = half(tile(arr, -step[d], 0, c), d)
            send(ref, ref, near_sent.at[0], s2r.at[c], yz[arr][d])

    def s2_wait(c):
        arrived(rl.at[0, 0, 0:2, c], s2r.at[c])

    def s3_send(c, k, sem):
        for d, arr in both:
            ref = tile(arr, off[k], 0, c)
            send(ref, ref, far_sent.at[0], s3r.at[sem], yz[1 - arr][d])

    def s4_send(c, k, sem):
        arrived(rl.at[0, 0, :, c], s3r.at[sem])
        for d, arr in both:
            ref = half(tile(arr, off[k], -step[d], c), d)
            send(ref, ref, far_sent.at[0], s4r.at[c], yz[1 - arr][d])

    def s3_line_send(c, sem):
        for d, arr in both:
            ref = line(arr, 0, c)
            send(ref, ref, far_sent.at[0], s3r.at[sem], yz[1 - arr][d])

    def s4_line_send(c, sem):
        arrived(rl.at[0, :, :, c], s3r.at[sem])
        for d, arr in both:
            ref = half(line(arr, -step[d], c), d)
            send(ref, ref, far_sent.at[0], s4r.at[c], yz[1 - arr][d])

    def s4_wait(c):
        arrived(rl.at[0, 0:2, :, c], s4r.at[c])

    def shard(dx, other=False):
        return wrap(x + dx) * 2 + (1 - core if other else core)

    def right_first():
        for arr, d in ((0, 0), (1, 1), (1, 0), (0, 1)):
            send((rth, rtl)[arr], rr.at[arr, row], right_sent.at[0], rv.at[arr * 2 + d], xs[d])
        for arr in (0, 1):
            send((rth, rtl)[arr], rr.at[arr, row], right_sent.at[0], rv.at[4], twin)

    def right_across(arr, dx, sem):
        ref = rr.at[arr, shard(dx)]
        send(ref, ref, right_sent.at[0], rv.at[sem], twin)

    def right_second(d):
        ref = rr.at[d, shard(-step[d])]
        arrived(ref, rv.at[d * 3])
        send(ref, ref, right_sent.at[0], rv.at[5 + d], xs[d])
        right_across(d, -step[d], 7 + d)

    def right_second_rest(d):
        arr = 1 - d
        arrived(rr.at[arr, shard(-step[d])], rv.at[arr * 2 + d])
        right_across(arr, -step[d], 7 + d)

    def right_third(d):
        arrived(rr.at[d, shard(2)], rv.at[5 + d])
        right_across(d, 2, 9)

    def right_crossed(dx, sem):
        arrived(rr.at[:, shard(dx, True)], rv.at[sem])
        split_right(shard(dx, True))

    def split_right(index):
        rows = pl.multiple_of(index * RD, RD)
        for arr, base in ((0, 1024), (1, 0)):
            high, low = split(rr[arr, index])
            b[pl.ds(base + rows, RD), :] = high
            b[pl.ds(base + 512 + rows, RD), :] = low

    s1_send(0)
    right_first()
    s3_send(0, 0, 0)
    for c in (1, 2, 3):
        pack(c)
        s1_send(c)
    for copy in own_right:
        copy.wait()
    split_right(row)
    s2_send(0)
    for k in (1, 2):
        s3_send(0, k, k)
    right_crossed(0, 4)
    s2_send(1)
    s2_wait(0)
    s3_send(0, 3, 3)
    for c in (2, 3):
        s2_send(c)
    s3_send(1, 0, 4)
    s4_send(0, 0, 0)
    for d in (0, 1):
        right_second(d)
    for k in (1, 2):
        s3_send(1, k, 4)
        s4_send(0, k, k)
    s2_wait(1)
    s3_send(1, 3, 4)
    for d in (0, 1):
        right_second_rest(d)
    s4_send(0, 3, 3)
    s2_wait(2)
    s3_line_send(2, 5)
    for d in (0, 1):
        split_right(shard(-step[d]))
    for d in (0, 1):
        right_crossed(-step[d], 7 + d)
    for d in (0, 1):
        right_third(d)
    split_right(shard(2))
    right_crossed(2, 9)
    s2_wait(3)

    lane = lax.broadcasted_iota(jnp.int32, (SUB, 128), 1) // KD

    def collect(c, target):
        def body(g, carry):
            for arr in (0, 1):
                for j in range(4):
                    value = rl[arr, g, (3 - j) % 4, c]
                    for p in range(3):
                        value = jnp.where(lane == p, rl[arr, g, (p - j) % 4, c], value)
                    if j:
                        value = pltpu.roll(value, 128 - KD * j, 1)
                    high, low = split(value)
                    cols = pl.multiple_of(arr * 1024 + g * 128, 128)
                    target[pl.ds(j * SUB, SUB), pl.ds(cols, 128)] = low
                    target[pl.ds(j * SUB, SUB), pl.ds(cols + 512, 128)] = high
            return carry

        lax.fori_loop(0, 4, body, 0)

    def multiply(c, u):
        src = pl.ds(u * 256, 256)
        dst = pl.ds(c * CH + u * 256, 256)
        out_h[dst, :] = times_hh(a, b, src)
        yield
        out_l[dst, :] = times_ll(a, b, src)
        yield
        out_c[dst, :] = times_cross(a, b, src)
        yield

    def chunk(c, events):
        collect(c, a)
        n = 0
        for u in (0, 1):
            for _ in multiply(c, u):
                if n in events:
                    events[n]()
                n += 1

    s4_wait(0)

    def second():
        s4_line_send(1, 4)
        s3_send(3, 0, 6)

    chunk(0, {2: second})
    s4_wait(1)

    def third():
        s4_line_send(2, 5)
        for k in (1, 2, 3):
            s3_send(3, k, 6 + k)

    chunk(1, {1: third})
    s4_wait(2)
    chunk(2, {k: functools.partial(s4_send, 3, k, 6 + k) for k in range(4)})
    s4_wait(3)
    collect(EARLY, a_last)
    arrived(rl.at[:, :, 0:3, 0], near_sent.at[0])
    arrived(rl.at[:, :, :, 0:3], far_sent.at[0])
    arrived(rr.at[:, 0:7], right_sent.at[0])


def finish_kernel(c_in, h_in, l_in, a, b, c_out, h_out, l_out, stage, early_sem, late_sem):
    copies = []
    for i, (src, dst) in enumerate(((c_in, c_out), (h_in, h_out), (l_in, l_out))):
        for q in range(EARLY):
            rows = pl.ds(q * CH, CH)
            copies.append(pltpu.make_async_copy(src.at[rows], dst.at[rows], early_sem.at[i, q]))
            copies[-1].start()
    for u in range(2):
        rows = pl.ds(u * 256, 256)
        for i, (times, dst) in enumerate(((times_cross, c_out), (times_hh, h_out), (times_ll, l_out))):
            stage[i, rows] = times(a, b, rows)
            copies.append(
                pltpu.make_async_copy(
                    stage.at[i, rows], dst.at[pl.ds(EARLY * CH + u * 256, 256)], late_sem.at[i, u]
                )
            )
            copies[-1].start()
    for copy in copies:
        copy.wait()


def per_device(left_h, left_l, right_h, right_l):
    dma = pltpu.SemaphoreType.DMA
    hbm, vmem = pl.BlockSpec(memory_space=pl.ANY), pl.BlockSpec(memory_space=pltpu.VMEM)
    early = pl.pallas_call(
        gather_kernel,
        out_shape=[pltpu.VMEM((EARLY * CH, N), F32)] * 3
        + [pltpu.VMEM((CH, 4 * KW), BF16), pltpu.VMEM((4 * KW, N), BF16)],
        in_specs=[hbm] * 4,
        out_specs=[vmem] * 5,
        scratch_shapes=[
            pltpu.VMEM((2, KD, M), F32),
            pltpu.VMEM((2, 4, 4, NCH, SUB, 128), F32),
            pltpu.VMEM((2, 8, RD, N), F32),
            pltpu.VMEM((CH, 4 * KW), BF16),
            dma((4,)),
            dma((1,)), dma((1,)), dma((1,)), dma((NCH,)), dma((NCH,)), dma((10,)), dma((NCH,)), dma((10,)),
        ],
        compiler_params=pltpu.CompilerParams(
            collective_id=0, has_side_effects=True, vmem_limit_bytes=22 << 20
        ),
        cost_estimate=pl.CostEstimate(flops=18 * M * N * KW, bytes_accessed=2 << 20, transcendentals=0),
        name="gather_multiply",
    )(*(pltpu.with_memory_space_constraint(v, pltpu.HBM) for v in (left_h.T, left_l.T, right_h, right_l)))
    return pl.pallas_call(
        finish_kernel,
        out_shape=[jax.ShapeDtypeStruct((M, N), F32)] * 3,
        in_specs=[vmem] * 5,
        out_specs=[hbm] * 3,
        scratch_shapes=[pltpu.VMEM((3, CH, N), F32), dma((3, EARLY)), dma((3, 2))],
        compiler_params=pltpu.CompilerParams(vmem_limit_bytes=10 << 20),
        cost_estimate=pl.CostEstimate(flops=6 * M * N * KW, bytes_accessed=24 << 20, transcendentals=0),
        name="multiply_write",
    )(*(pltpu.with_memory_space_constraint(v, pltpu.VMEM) for v in early))


def solution(mesh):
    spec = P("row", "col")
    return jax.shard_map(
        per_device, mesh=mesh, in_specs=(spec,) * 4, out_specs=(spec,) * 3, check_vma=False
    )
```

```python
import functools

import jax
import jax.numpy as jnp
from jax import lax
from jax.experimental import pallas as pl
from jax.experimental.pallas import tpu as pltpu
from jax.sharding import PartitionSpec as P

KW = 512
SCALE = 2.0**30 / KW
MESH = pl.DeviceIdType.MESH
F32, BF16 = jnp.float32, jnp.bfloat16

M, N, KD, RD = 2048, 1024, 32, 64
CH = 512
NCH = M // CH
SUB = CH // 4
BLK = 32
LATE = CH
EARLY = M - LATE

dot = functools.partial(jnp.dot, preferred_element_type=F32)


def split(value):
    high = value.astype(BF16)
    return high, (value - high.astype(F32)).astype(BF16)


def times_hh(a, b, rows):
    return SCALE * (dot(a[rows, 0:1024], b[1024:2048, :]) + dot(a[rows, 512:1024], b[1024:1536, :]))


def times_ll(a, b, rows):
    return SCALE * (dot(a[rows, 1024:2048], b[0:1024, :]) + dot(a[rows, 1536:2048], b[0:512, :]))


def times_cross(a, b, rows):
    small = dot(a[rows, :], b[:, :])
    return SCALE * (small + (dot(a[rows, 512:1024], b[0:512, :]) + dot(a[rows, 1536:2048], b[1024:1536, :])))


def collect(tiles, target):
    lane = lax.broadcasted_iota(jnp.int32, (BLK, 128), 1) // KD

    def body(g, carry):
        for arr in (0, 1):
            cols = pl.multiple_of(arr * 1024 + g * 128, 128)
            for r in range(0, SUB, BLK):
                source = [tiles[arr, g, q, pl.ds(r, BLK)] for q in range(4)]
                for j in range(4):
                    value = source[(3 - j) % 4]
                    for p in range(3):
                        value = jnp.where(lane == p, source[(p - j) % 4], value)
                    if j:
                        value = pltpu.roll(value, 128 - KD * j, 1)
                    high, low = split(value)
                    rows = pl.ds(j * SUB + r, BLK)
                    target[rows, pl.ds(cols, 128)] = low
                    target[rows, pl.ds(cols + 512, 128)] = high
        return carry

    lax.fori_loop(0, 4, body, 0)


def gather_kernel(
    lth, ltl, rth, rtl,
    out_c, out_h, out_l, rl_last, b,
    lt, rl, rr, a, load_sem,
    near_sent, far_sent, right_sent, s1r, s2r, s3r, s4r, rv,
):
    row, col = lax.axis_index("row"), lax.axis_index("col")
    x, core, y, z = row // 2, row % 2, col // 4, col % 4

    def wrap(v):
        return lax.rem(v + 8, 4)

    def at(dx=0, dc=0, dy=0, dz=0):
        new_core = 1 - core if dc else core
        return (wrap(x + dx) * 2 + new_core, wrap(y + dy) * 4 + wrap(z + dz))

    step = (1, -1)
    yz = tuple(tuple(at(dy=d) if ax == 0 else at(dz=d) for d in step) for ax in (0, 1))
    xs = tuple(at(dx=d) for d in step)
    twin = at(dc=1)

    loads = [pltpu.make_async_copy(ref, lt.at[i], load_sem.at[i]) for i, ref in enumerate((lth, ltl))]
    own_right = [pltpu.make_async_copy(ref, rr.at[i, row], load_sem.at[2 + i]) for i, ref in enumerate((rth, rtl))]
    for copy in loads + own_right:
        copy.start()
    barrier = pltpu.get_barrier_semaphore()
    for device in (*yz[0], *yz[1], *xs, twin):
        pl.semaphore_signal(barrier, 1, device_id=device, device_id_type=MESH)
    for copy in loads:
        copy.wait()

    def chunk(c):
        return rl_last if c == NCH - 1 else rl.at[c]

    def pack(c):
        for arr in (0, 1):
            parts = []
            for p in range(4):
                start = pl.multiple_of(c * CH + wrap(p - z) * SUB, SUB)
                parts.append(lt[arr, :, pl.ds(start, SUB)])
            chunk(c)[arr, y, z] = jnp.concatenate(parts, axis=0).T

    pack(0)
    pl.semaphore_wait(barrier, 7)

    def send(src, dst, send_sem, recv_sem, device):
        pltpu.make_async_remote_copy(
            src_ref=src, dst_ref=dst, send_sem=send_sem, recv_sem=recv_sem, device_id=device, device_id_type=MESH
        ).start()

    def arrived(ref, sem):
        pltpu.make_async_copy(ref, ref, sem).wait()

    off = (0, -1, 1, 2)
    both = [(d, arr) for d in (0, 1) for arr in (0, 1)]

    def tile(arr, first, second, c):
        f, s = wrap((y, z)[arr] + first), wrap((z, y)[arr] + second)
        return chunk(c).at[arr, f, s] if arr == 0 else chunk(c).at[arr, s, f]

    def half(ref, d):
        return ref.at[pl.ds(d * (SUB // 2), SUB // 2)]

    def s1_send(c):
        for d, arr in both:
            ref = tile(arr, 0, 0, c)
            send(ref, ref, near_sent.at[0], s1r.at[c], yz[arr][d])

    def s2_send(c):
        arrived(rl.at[0, 0, 0], s1r.at[c])
        for d, arr in both:
            ref = half(tile(arr, -step[d], 0, c), d)
            send(ref, ref, near_sent.at[0], s2r.at[c], yz[arr][d])

    def s2_wait(c):
        arrived(rl.at[0, 0, 0, 0:2], s2r.at[c])

    def s3_send(c, *ks):
        for k in ks:
            for d, arr in both:
                ref = tile(arr, off[k], 0, c)
                send(ref, ref, far_sent.at[0], s3r.at[c, k], yz[1 - arr][d])

    def s4_send(c, *ks):
        for k in ks:
            arrived(rl.at[0, 0, 0], s3r.at[c, k])
            for d, arr in both:
                ref = half(tile(arr, off[k], -step[d], c), d)
                send(ref, ref, far_sent.at[0], s4r.at[c], yz[1 - arr][d])

    def s4_wait(c):
        arrived(rl.at[0, 0, 0:2], s4r.at[c])

    def shard(dx, other=False):
        return wrap(x + dx) * 2 + (1 - core if other else core)

    def right_first():
        for arr, d in ((0, 0), (1, 1), (1, 0), (0, 1)):
            send((rth, rtl)[arr], rr.at[arr, row], right_sent.at[0], rv.at[arr * 2 + d], xs[d])
        for arr in (0, 1):
            send((rth, rtl)[arr], rr.at[arr, row], right_sent.at[0], rv.at[4], twin)

    def right_across(arr, dx, sem):
        ref = rr.at[arr, shard(dx)]
        send(ref, ref, right_sent.at[0], rv.at[sem], twin)

    def right_second(d):
        ref = rr.at[d, shard(-step[d])]
        arrived(ref, rv.at[d * 3])
        send(ref, ref, right_sent.at[0], rv.at[5 + d], xs[d])
        right_across(d, -step[d], 7 + d)

    def right_second_rest(d):
        arr = 1 - d
        arrived(rr.at[arr, shard(-step[d])], rv.at[arr * 2 + d])
        right_across(arr, -step[d], 7 + d)

    def right_third(d):
        arrived(rr.at[d, shard(2)], rv.at[5 + d])
        right_across(d, 2, 9)

    def right_crossed(dx, sem):
        arrived(rr.at[:, shard(dx, True)], rv.at[sem])
        split_right(shard(dx, True))

    def split_right(index):
        rows = pl.multiple_of(index * RD, RD)
        for arr, base in ((0, 1024), (1, 0)):
            high, low = split(rr[arr, index])
            b[pl.ds(base + rows, RD), :] = high
            b[pl.ds(base + 512 + rows, RD), :] = low

    s1_send(0)
    right_first()
    s3_send(0, 0)
    pack(1)
    s1_send(1)
    pack(2)
    pack(3)
    for copy in own_right:
        copy.wait()
    split_right(row)
    s2_send(0)
    s3_send(0, 1, 2)
    s1_send(2)
    right_crossed(0, 4)
    s2_wait(0)
    s3_send(0, 3)
    s2_send(1)
    s4_send(0, 0)
    for d in (0, 1):
        right_second(d)
    s4_send(0, 1, 2)
    s3_send(1, 0)
    s2_send(2)
    s4_send(0, 3)
    s3_send(1, 1, 2)
    s2_wait(1)
    s3_send(1, 3)
    s1_send(3)
    s3_send(2, 0)
    for d in (0, 1):
        right_second_rest(d)
    for d in (0, 1):
        split_right(shard(-step[d]))
    for d in (0, 1):
        right_crossed(-step[d], 7 + d)
    s4_send(1, 0)
    s4_wait(0)
    collect(rl.at[0], a)
    for d in (0, 1):
        right_third(d)
    split_right(shard(2))
    right_crossed(2, 9)
    s2_wait(2)

    def multiply(start, events):
        n = 0
        for u in range(0, CH, 256):
            src, dst = pl.ds(u, 256), pl.ds(start + u, 256)
            for out, times in ((out_h, times_hh), (out_l, times_ll), (out_c, times_cross)):
                out[dst, :] = times(a, b, src)
                for step_, *given in events.get(n, ()):
                    step_(*given)
                n += 1

    multiply(
        0,
        {
            1: ((s4_send, 1, 1, 2),),
            2: ((s4_send, 1, 3), (s3_send, 2, 1, 2, 3)),
            3: ((s2_send, 3), (s3_send, 3, 0)),
        },
    )
    s4_wait(1)
    collect(rl.at[1], a)
    multiply(
        CH,
        {
            1: ((s4_send, 2, 0, 1),),
            2: ((s4_send, 2, 2, 3), (s3_send, 3, 1, 2)),
            3: ((s2_wait, 3), (s3_send, 3, 3)),
            5: ((s4_send, 3, 0),),
        },
    )
    s4_wait(2)
    collect(rl.at[2], a)
    multiply(2 * CH, {0: ((s4_send, 3, 1),), 1: ((s4_send, 3, 2),), 2: ((s4_send, 3, 3),)})
    s4_wait(3)
    arrived(rl.at[0, :, :, 0:3], near_sent.at[0])
    arrived(rl, far_sent.at[0])
    arrived(rr.at[:, 0:7], right_sent.at[0])


def finish_kernel(c_in, h_in, l_in, tiles, b, c_out, h_out, l_out, a, stage, early_sem, late_sem):
    copies = []
    for i, (src, dst) in enumerate(((c_in, c_out), (h_in, h_out), (l_in, l_out))):
        for q, start in enumerate(range(0, EARLY, CH)):
            rows = pl.ds(start, min(CH, EARLY - start))
            copies.append(pltpu.make_async_copy(src.at[rows], dst.at[rows], early_sem.at[i, q]))
            copies[-1].start()
    collect(tiles, a)
    for u in range(2):
        rows = pl.ds(u * (LATE // 2), LATE // 2)
        for i, (times, dst) in enumerate(((times_cross, c_out), (times_hh, h_out), (times_ll, l_out))):
            stage[i, rows] = times(a, b, rows)
            copies.append(
                pltpu.make_async_copy(
                    stage.at[i, rows], dst.at[pl.ds(EARLY + u * (LATE // 2), LATE // 2)], late_sem.at[i, u]
                )
            )
            copies[-1].start()
    for copy in copies:
        copy.wait()


def per_device(left_h, left_l, right_h, right_l):
    dma = pltpu.SemaphoreType.DMA
    hbm, vmem = pl.BlockSpec(memory_space=pl.ANY), pl.BlockSpec(memory_space=pltpu.VMEM)
    early = pl.pallas_call(
        gather_kernel,
        out_shape=[pltpu.VMEM((EARLY, N), F32)] * 3
        + [pltpu.VMEM((2, 4, 4, SUB, 128), F32), pltpu.VMEM((4 * KW, N), BF16)],
        in_specs=[hbm] * 4,
        out_specs=[vmem] * 5,
        scratch_shapes=[
            pltpu.VMEM((2, KD, M), F32),
            pltpu.VMEM((NCH - 1, 2, 4, 4, SUB, 128), F32),
            pltpu.VMEM((2, 8, RD, N), F32),
            pltpu.VMEM((CH, 4 * KW), BF16),
            dma((4,)),
            dma((1,)), dma((1,)), dma((1,)), dma((NCH,)), dma((NCH,)), dma((NCH, 4)), dma((NCH,)), dma((10,)),
        ],
        compiler_params=pltpu.CompilerParams(
            collective_id=0, has_side_effects=True, vmem_limit_bytes=22 << 20
        ),
        cost_estimate=pl.CostEstimate(flops=24 * EARLY * N * KW, bytes_accessed=2 << 20, transcendentals=0),
        name="gather_multiply",
    )(*(pltpu.with_memory_space_constraint(v, pltpu.HBM) for v in (left_h.T, left_l.T, right_h, right_l)))
    return pl.pallas_call(
        finish_kernel,
        out_shape=[jax.ShapeDtypeStruct((M, N), F32)] * 3,
        in_specs=[vmem] * 5,
        out_specs=[hbm] * 3,
        scratch_shapes=[pltpu.VMEM((LATE, 4 * KW), BF16), pltpu.VMEM((3, LATE, N), F32), dma((3, 3)), dma((3, 2))],
        compiler_params=pltpu.CompilerParams(vmem_limit_bytes=12 << 20),
        cost_estimate=pl.CostEstimate(flops=24 * LATE * N * KW, bytes_accessed=24 << 20, transcendentals=0),
        name="multiply_write",
    )(*(pltpu.with_memory_space_constraint(v, pltpu.VMEM) for v in early))


def solution(mesh):
    spec = P("row", "col")
    return jax.shard_map(
        per_device, mesh=mesh, in_specs=(spec,) * 4, out_specs=(spec,) * 3, check_vma=False
    )
```

```python
import functools

import jax
import jax.numpy as jnp
from jax import lax
from jax.experimental import pallas as pl
from jax.experimental.pallas import tpu as pltpu
from jax.sharding import PartitionSpec as P

KW = 512
SCALE = 2.0**30 / KW
MESH = pl.DeviceIdType.MESH
F32, BF16 = jnp.float32, jnp.bfloat16

M, N, KD, RD = 2048, 1024, 32, 64
CH = 512
NCH = M // CH
SUB = CH // 4
BLK = 32
LATE = CH
EARLY = M - LATE

dot = functools.partial(jnp.dot, preferred_element_type=F32)


def split(value):
    high = value.astype(BF16)
    return high, (value - high.astype(F32)).astype(BF16)


def times_hh(a, b, rows):
    return SCALE * (dot(a[rows, 0:1024], b[1024:2048, :]) + dot(a[rows, 512:1024], b[1024:1536, :]))


def times_ll(a, b, rows):
    return SCALE * (dot(a[rows, 1024:2048], b[0:1024, :]) + dot(a[rows, 1536:2048], b[0:512, :]))


def times_cross(a, b, rows):
    small = dot(a[rows, :], b[:, :])
    return SCALE * (small + (dot(a[rows, 512:1024], b[0:512, :]) + dot(a[rows, 1536:2048], b[1024:1536, :])))


def times_part(a, b, rows, start, left, right):
    low, high = a[rows, pl.ds(left + start, 256)], a[rows, pl.ds(left + 512 + start, 256)]
    b_high, b_low = b[pl.ds(right + start, 256), :], b[pl.ds(right + 512 + start, 256), :]
    return dot(low, b_high) + dot(high, b_low) + dot(high, b_high)


def collect(tiles, target):
    lane = lax.broadcasted_iota(jnp.int32, (BLK, 128), 1) // KD

    def body(g, carry):
        for arr in (0, 1):
            cols = pl.multiple_of(arr * 1024 + g * 128, 128)
            for r in range(0, SUB, BLK):
                source = [tiles[arr, g, q, pl.ds(r, BLK)] for q in range(4)]
                for j in range(4):
                    value = source[(3 - j) % 4]
                    for p in range(3):
                        value = jnp.where(lane == p, source[(p - j) % 4], value)
                    if j:
                        value = pltpu.roll(value, 128 - KD * j, 1)
                    high, low = split(value)
                    rows = pl.ds(j * SUB + r, BLK)
                    target[rows, pl.ds(cols, 128)] = low
                    target[rows, pl.ds(cols + 512, 128)] = high
        return carry

    lax.fori_loop(0, 4, body, 0)


def gather_kernel(
    lth, ltl, rth, rtl,
    out_c, out_h, out_l, rl_last, b,
    lt, rl, rr, a, load_sem,
    near_sent, far_sent, right_sent, s1r, s2r, s3r, s4r, rv,
):
    row, col = lax.axis_index("row"), lax.axis_index("col")
    x, core, y, z = row // 2, row % 2, col // 4, col % 4

    def wrap(v):
        return lax.rem(v + 8, 4)

    def at(dx=0, dc=0, dy=0, dz=0):
        new_core = 1 - core if dc else core
        return (wrap(x + dx) * 2 + new_core, wrap(y + dy) * 4 + wrap(z + dz))

    step = (1, -1)
    yz = tuple(tuple(at(dy=d) if ax == 0 else at(dz=d) for d in step) for ax in (0, 1))
    xs = tuple(at(dx=d) for d in step)
    twin = at(dc=1)

    loads = [pltpu.make_async_copy(ref, lt.at[i], load_sem.at[i]) for i, ref in enumerate((lth, ltl))]
    own_right = [pltpu.make_async_copy(ref, rr.at[i, row], load_sem.at[2 + i]) for i, ref in enumerate((rth, rtl))]
    for copy in loads + own_right:
        copy.start()
    barrier = pltpu.get_barrier_semaphore()
    for device in (*yz[0], *yz[1], *xs, twin):
        pl.semaphore_signal(barrier, 1, device_id=device, device_id_type=MESH)
    for copy in loads:
        copy.wait()

    def chunk(c):
        return rl_last if c == NCH - 1 else rl.at[c]

    def pack(c):
        for arr in (0, 1):
            parts = []
            for p in range(4):
                start = pl.multiple_of(c * CH + wrap(p - z) * SUB, SUB)
                parts.append(lt[arr, :, pl.ds(start, SUB)])
            chunk(c)[arr, y, z] = jnp.concatenate(parts, axis=0).T

    pack(0)
    pl.semaphore_wait(barrier, 7)

    def send(src, dst, send_sem, recv_sem, device):
        pltpu.make_async_remote_copy(
            src_ref=src, dst_ref=dst, send_sem=send_sem, recv_sem=recv_sem, device_id=device, device_id_type=MESH
        ).start()

    def arrived(ref, sem):
        pltpu.make_async_copy(ref, ref, sem).wait()

    off = (0, -1, 1, 2)
    both = [(d, arr) for d in (0, 1) for arr in (0, 1)]

    def tile(arr, first, second, c):
        f, s = wrap((y, z)[arr] + first), wrap((z, y)[arr] + second)
        return chunk(c).at[arr, f, s] if arr == 0 else chunk(c).at[arr, s, f]

    def half(ref, d):
        return ref.at[pl.ds(d * (SUB // 2), SUB // 2)]

    def s1_send(c):
        for d, arr in both:
            ref = tile(arr, 0, 0, c)
            send(ref, ref, near_sent.at[0], s1r.at[c], yz[arr][d])

    def s2_send(c):
        arrived(rl.at[0, 0, 0], s1r.at[c])
        for d, arr in both:
            ref = half(tile(arr, -step[d], 0, c), d)
            send(ref, ref, near_sent.at[0], s2r.at[c], yz[arr][d])

    def s2_wait(c):
        arrived(rl.at[0, 0, 0, 0:2], s2r.at[c])

    def s3_send(c, *ks):
        for k in ks:
            for d, arr in both:
                ref = tile(arr, off[k], 0, c)
                send(ref, ref, far_sent.at[0], s3r.at[c, k], yz[1 - arr][d])

    def s4_send(c, *ks):
        for k in ks:
            arrived(rl.at[0, 0, 0], s3r.at[c, k])
            for d, arr in both:
                ref = half(tile(arr, off[k], -step[d], c), d)
                send(ref, ref, far_sent.at[0], s4r.at[c], yz[1 - arr][d])

    def s4_wait(c):
        arrived(rl.at[0, 0, 0:2], s4r.at[c])

    def shard(dx, other=False):
        return wrap(x + dx) * 2 + (1 - core if other else core)

    def right_first():
        for arr, d in ((0, 0), (1, 1), (1, 0), (0, 1)):
            send((rth, rtl)[arr], rr.at[arr, row], right_sent.at[0], rv.at[arr * 2 + d], xs[d])
        for arr in (0, 1):
            send((rth, rtl)[arr], rr.at[arr, row], right_sent.at[0], rv.at[4], twin)

    def right_across(arr, dx, sem):
        ref = rr.at[arr, shard(dx)]
        send(ref, ref, right_sent.at[0], rv.at[sem], twin)

    def right_second(d):
        ref = rr.at[d, shard(-step[d])]
        arrived(ref, rv.at[d * 3])
        send(ref, ref, right_sent.at[0], rv.at[5 + d], xs[d])
        right_across(d, -step[d], 7 + d)

    def right_second_rest(d):
        arr = 1 - d
        arrived(rr.at[arr, shard(-step[d])], rv.at[arr * 2 + d])
        right_across(arr, -step[d], 7 + d)

    def right_third(d):
        arrived(rr.at[d, shard(2)], rv.at[5 + d])
        right_across(d, 2, 9)

    def right_crossed(dx, sem):
        arrived(rr.at[:, shard(dx, True)], rv.at[sem])
        split_right(shard(dx, True))

    def split_right(index):
        rows = pl.multiple_of(index * RD, RD)
        for arr, base in ((0, 1024), (1, 0)):
            high, low = split(rr[arr, index])
            b[pl.ds(base + rows, RD), :] = high
            b[pl.ds(base + 512 + rows, RD), :] = low

    s1_send(0)
    right_first()
    s3_send(0, 0)
    pack(1)
    s1_send(1)
    pack(2)
    pack(3)
    for copy in own_right:
        copy.wait()
    split_right(row)
    s2_send(0)
    s3_send(0, 1, 2)
    s1_send(2)
    right_crossed(0, 4)
    s2_wait(0)
    s3_send(0, 3)
    s2_send(1)
    s4_send(0, 0)
    for d in (0, 1):
        right_second(d)
    s4_send(0, 1, 2)
    s3_send(1, 0)
    s2_send(2)
    s4_send(0, 3)
    s3_send(1, 1, 2)
    s2_wait(1)
    s3_send(1, 3)
    s1_send(3)
    s3_send(2, 0)
    for d in (0, 1):
        right_second_rest(d)
    for d in (0, 1):
        split_right(shard(-step[d]))
    for d in (0, 1):
        right_crossed(-step[d], 7 + d)
    s4_send(1, 0)
    s4_wait(0)
    collect(rl.at[0], a)

    def after(events, n):
        for step_, *given in events.get(n, ()):
            step_(*given)

    def after_by_core(events, n):
        if len(events) == 1 or events[0].get(n) == events[1].get(n):
            return after(events[0], n)
        for which in (0, 1):
            if n in events[which]:
                pl.when(core == which)(functools.partial(after, events[which], n))

    def multiply(start, *events):
        n = 0
        for u in range(0, CH, 256):
            src, dst = pl.ds(u, 256), pl.ds(start + u, 256)
            for out, times in ((out_h, times_hh), (out_l, times_ll), (out_c, times_cross)):
                out[dst, :] = times(a, b, src)
                after_by_core(events, n)
                n += 1

    def multiply_part(index, more, events):
        start = pl.multiple_of(index * 256, 256)
        n = 0
        for u in range(0, CH, 256):
            rows = pl.ds(u, 256)
            for out, terms in (
                (out_h, ((0, 1024),)),
                (out_l, ((1024, 0),)),
                (out_c, ((0, 0), (1024, 1024))),
            ):
                value = SCALE * sum(times_part(a, b, rows, start, *term) for term in terms)
                out[rows, :] = out[rows, :] + value if more else value
                after(events, n)
                n += 1

    multiply_part(x // 2, False, {1: ((right_third, 0), (right_third, 1))})
    s4_send(1, 1, 2)
    split_right(shard(2))
    right_crossed(2, 9)
    multiply_part(
        1 - x // 2,
        True,
        {
            1: ((s4_send, 1, 3), (s2_wait, 2), (s3_send, 2, 1, 2, 3)),
            3: ((s2_send, 3), (s3_send, 3, 0)),
        },
    )
    s4_wait(1)
    collect(rl.at[1], a)
    multiply(
        CH,
        {
            1: ((s4_send, 2, 0, 1),),
            2: ((s4_send, 2, 2, 3), (s3_send, 3, 1, 2)),
            3: ((s2_wait, 3), (s3_send, 3, 3)),
            5: ((s4_send, 3, 0),),
        },
        {2: ((s4_send, 2, 0, 1),), 3: ((s4_send, 2, 2, 3), (s2_wait, 3)), 4: ((s3_send, 3, 1),), 5: ((s3_send, 3, 2, 3),)},
    )
    s4_wait(2)
    collect(rl.at[2], a)
    multiply(
        2 * CH,
        {0: ((s4_send, 3, 1),), 1: ((s4_send, 3, 2),), 2: ((s4_send, 3, 3),)},
        {1: ((s4_send, 3, 0, 1),), 2: ((s4_send, 3, 2),), 3: ((s4_send, 3, 3),)},
    )
    s4_wait(3)
    arrived(rl.at[0, :, :, 0:3], near_sent.at[0])
    arrived(rl, far_sent.at[0])
    arrived(rr.at[:, 0:7], right_sent.at[0])


def finish_kernel(c_in, h_in, l_in, tiles, b, c_out, h_out, l_out, a, stage, early_sem, late_sem):
    copies = []
    for i, (src, dst) in enumerate(((c_in, c_out), (h_in, h_out), (l_in, l_out))):
        for q, start in enumerate(range(0, EARLY, CH)):
            rows = pl.ds(start, min(CH, EARLY - start))
            copies.append(pltpu.make_async_copy(src.at[rows], dst.at[rows], early_sem.at[i, q]))
            copies[-1].start()
    collect(tiles, a)
    for u in range(2):
        rows = pl.ds(u * (LATE // 2), LATE // 2)
        for i, (times, dst) in enumerate(((times_cross, c_out), (times_hh, h_out), (times_ll, l_out))):
            stage[i, rows] = times(a, b, rows)
            copies.append(
                pltpu.make_async_copy(
                    stage.at[i, rows], dst.at[pl.ds(EARLY + u * (LATE // 2), LATE // 2)], late_sem.at[i, u]
                )
            )
            copies[-1].start()
    for copy in copies:
        copy.wait()


def per_device(left_h, left_l, right_h, right_l):
    dma = pltpu.SemaphoreType.DMA
    hbm, vmem = pl.BlockSpec(memory_space=pl.ANY), pl.BlockSpec(memory_space=pltpu.VMEM)
    early = pl.pallas_call(
        gather_kernel,
        out_shape=[pltpu.VMEM((EARLY, N), F32)] * 3
        + [pltpu.VMEM((2, 4, 4, SUB, 128), F32), pltpu.VMEM((4 * KW, N), BF16)],
        in_specs=[hbm] * 4,
        out_specs=[vmem] * 5,
        scratch_shapes=[
            pltpu.VMEM((2, KD, M), F32),
            pltpu.VMEM((NCH - 1, 2, 4, 4, SUB, 128), F32),
            pltpu.VMEM((2, 8, RD, N), F32),
            pltpu.VMEM((CH, 4 * KW), BF16),
            dma((4,)),
            dma((1,)), dma((1,)), dma((1,)), dma((NCH,)), dma((NCH,)), dma((NCH, 4)), dma((NCH,)), dma((10,)),
        ],
        compiler_params=pltpu.CompilerParams(
            collective_id=0, has_side_effects=True, vmem_limit_bytes=22 << 20
        ),
        cost_estimate=pl.CostEstimate(flops=24 * EARLY * N * KW, bytes_accessed=2 << 20, transcendentals=0),
        name="gather_multiply",
    )(*(pltpu.with_memory_space_constraint(v, pltpu.HBM) for v in (left_h.T, left_l.T, right_h, right_l)))
    return pl.pallas_call(
        finish_kernel,
        out_shape=[jax.ShapeDtypeStruct((M, N), F32)] * 3,
        in_specs=[vmem] * 5,
        out_specs=[hbm] * 3,
        scratch_shapes=[pltpu.VMEM((LATE, 4 * KW), BF16), pltpu.VMEM((3, LATE, N), F32), dma((3, 3)), dma((3, 2))],
        compiler_params=pltpu.CompilerParams(vmem_limit_bytes=12 << 20),
        cost_estimate=pl.CostEstimate(flops=24 * LATE * N * KW, bytes_accessed=24 << 20, transcendentals=0),
        name="multiply_write",
    )(*(pltpu.with_memory_space_constraint(v, pltpu.VMEM) for v in early))


def solution(mesh):
    spec = P("row", "col")
    return jax.shard_map(
        per_device, mesh=mesh, in_specs=(spec,) * 4, out_specs=(spec,) * 3, check_vma=False
    )
```

```python
import functools

import jax
import jax.numpy as jnp
from jax import lax
from jax.experimental import pallas as pl
from jax.experimental.pallas import tpu as pltpu
from jax.sharding import PartitionSpec as P

KW = 512
SCALE = 2.0**30 / KW
MESH = pl.DeviceIdType.MESH
F32, BF16 = jnp.float32, jnp.bfloat16

M, N, KD, RD = 2048, 1024, 32, 64
CH = 512
NCH = M // CH
SUB = CH // 4
BLK = 32
LATE = CH
EARLY = M - LATE

dot = functools.partial(jnp.dot, preferred_element_type=F32)


def split(value):
    high = value.astype(BF16)
    return high, (value - high.astype(F32)).astype(BF16)


def times_hh(a, b, rows):
    return SCALE * (dot(a[rows, 0:1024], b[1024:2048, :]) + dot(a[rows, 512:1024], b[1024:1536, :]))


def times_ll(a, b, rows):
    return SCALE * (dot(a[rows, 1024:2048], b[0:1024, :]) + dot(a[rows, 1536:2048], b[0:512, :]))


def times_cross(a, b, rows):
    small = dot(a[rows, :], b[:, :])
    return SCALE * (small + (dot(a[rows, 512:1024], b[0:512, :]) + dot(a[rows, 1536:2048], b[1024:1536, :])))


def times_part(a, b, rows, start, left, right):
    low, high = a[rows, pl.ds(left + start, 256)], a[rows, pl.ds(left + 512 + start, 256)]
    b_high, b_low = b[pl.ds(right + start, 256), :], b[pl.ds(right + 512 + start, 256), :]
    return dot(low, b_high) + dot(high, b_low) + dot(high, b_high)


def collect(tiles, target):
    lane = lax.broadcasted_iota(jnp.int32, (BLK, 128), 1) // KD

    def body(g, carry):
        for arr in (0, 1):
            cols = pl.multiple_of(arr * 1024 + g * 128, 128)
            for r in range(0, SUB, BLK):
                source = [tiles[arr, g, q, pl.ds(r, BLK)] for q in range(4)]
                for j in range(4):
                    value = source[(3 - j) % 4]
                    for p in range(3):
                        value = jnp.where(lane == p, source[(p - j) % 4], value)
                    if j:
                        value = pltpu.roll(value, 128 - KD * j, 1)
                    high, low = split(value)
                    rows = pl.ds(j * SUB + r, BLK)
                    target[rows, pl.ds(cols, 128)] = low
                    target[rows, pl.ds(cols + 512, 128)] = high
        return carry

    lax.fori_loop(0, 4, body, 0)


def gather_kernel(
    lth, ltl, rth, rtl,
    out_c, out_h, out_l, rl_last, b,
    lt, rl, rr, a, load_sem,
    near_sent, far_sent, right_sent, s1r, s2r, s3r, s4r, rv,
):
    row, col = lax.axis_index("row"), lax.axis_index("col")
    x, core, y, z = row // 2, row % 2, col // 4, col % 4

    def wrap(v):
        return lax.rem(v + 8, 4)

    def at(dx=0, dc=0, dy=0, dz=0):
        new_core = 1 - core if dc else core
        return (wrap(x + dx) * 2 + new_core, wrap(y + dy) * 4 + wrap(z + dz))

    step = (1, -1)
    yz = tuple(tuple(at(dy=d) if ax == 0 else at(dz=d) for d in step) for ax in (0, 1))
    xs = tuple(at(dx=d) for d in step)
    twin = at(dc=1)

    barrier = pltpu.get_barrier_semaphore()
    for device in (*yz[0], *yz[1], *xs, twin):
        pl.semaphore_signal(barrier, 1, device_id=device, device_id_type=MESH)
    for i, ref in enumerate((lth, ltl)):
        pltpu.make_async_copy(ref, lt.at[i], load_sem.at[0]).start()
    for i, ref in enumerate((rth, rtl)):
        pltpu.make_async_copy(ref, rr.at[i, row], load_sem.at[1]).start()
    pltpu.make_async_copy(lt, lt, load_sem.at[0]).wait()

    def chunk(c):
        return rl_last if c == NCH - 1 else rl.at[c]

    def pack(c):
        for arr in (0, 1):
            parts = []
            for p in range(4):
                start = pl.multiple_of(c * CH + wrap(p - z) * SUB, SUB)
                parts.append(lt[arr, :, pl.ds(start, SUB)])
            chunk(c)[arr, y, z] = jnp.concatenate(parts, axis=0).T

    pack(0)
    pl.semaphore_wait(barrier, 7)

    def send(src, dst, send_sem, recv_sem, device):
        pltpu.make_async_remote_copy(
            src_ref=src, dst_ref=dst, send_sem=send_sem, recv_sem=recv_sem, device_id=device, device_id_type=MESH
        ).start()

    def arrived(ref, sem):
        pltpu.make_async_copy(ref, ref, sem).wait()

    off = (0, -1, 1, 2)
    both = [(d, arr) for d in (0, 1) for arr in (0, 1)]

    def tile(arr, first, second, c):
        f, s = wrap((y, z)[arr] + first), wrap((z, y)[arr] + second)
        return chunk(c).at[arr, f, s] if arr == 0 else chunk(c).at[arr, s, f]

    def half(ref, d):
        return ref.at[pl.ds(d * (SUB // 2), SUB // 2)]

    def s1_send(c):
        for d, arr in both:
            ref = tile(arr, 0, 0, c)
            send(ref, ref, near_sent.at[0], s1r.at[c], yz[arr][d])

    def s2_send(c):
        arrived(rl.at[0, 0, 0], s1r.at[c])
        for d, arr in both:
            ref = half(tile(arr, -step[d], 0, c), d)
            send(ref, ref, near_sent.at[0], s2r.at[c], yz[arr][d])

    def s2_wait(c):
        arrived(rl.at[0, 0, 0, 0:2], s2r.at[c])

    def s3_send(c, *ks):
        for k in ks:
            for d, arr in both:
                ref = tile(arr, off[k], 0, c)
                send(ref, ref, far_sent.at[0], s3r.at[c, k], yz[1 - arr][d])

    def s4_send(c, *ks):
        for k in ks:
            arrived(rl.at[0, 0, 0], s3r.at[c, k])
            for d, arr in both:
                ref = half(tile(arr, off[k], -step[d], c), d)
                send(ref, ref, far_sent.at[0], s4r.at[c], yz[1 - arr][d])

    def s4_wait(c):
        arrived(rl.at[0, 0, 0:2], s4r.at[c])

    def shard(dx, other=False):
        return wrap(x + dx) * 2 + (1 - core if other else core)

    def right_first():
        for arr, d in ((0, 0), (1, 1), (1, 0), (0, 1)):
            send((rth, rtl)[arr], rr.at[arr, row], right_sent.at[0], rv.at[arr * 2 + d], xs[d])
        for arr in (0, 1):
            send((rth, rtl)[arr], rr.at[arr, row], right_sent.at[0], rv.at[4], twin)

    def right_across(arr, dx, sem):
        ref = rr.at[arr, shard(dx)]
        send(ref, ref, right_sent.at[0], rv.at[sem], twin)

    def right_second(d):
        ref = rr.at[d, shard(-step[d])]
        arrived(ref, rv.at[d * 3])
        send(ref, ref, right_sent.at[0], rv.at[5 + d], xs[d])
        right_across(d, -step[d], 7 + d)

    def right_second_rest(d):
        arr = 1 - d
        arrived(rr.at[arr, shard(-step[d])], rv.at[arr * 2 + d])
        right_across(arr, -step[d], 7 + d)

    def right_third(d):
        arrived(rr.at[d, shard(2)], rv.at[5 + d])
        right_across(d, 2, 9)

    def right_crossed(dx, sem):
        arrived(rr.at[:, shard(dx, True)], rv.at[sem])
        split_right(shard(dx, True))

    def split_right(index):
        rows = pl.multiple_of(index * RD, RD)
        for arr, base in ((0, 1024), (1, 0)):
            high, low = split(rr[arr, index])
            b[pl.ds(base + rows, RD), :] = high
            b[pl.ds(base + 512 + rows, RD), :] = low

    s1_send(0)
    right_first()
    s3_send(0, 0)
    pack(1)
    s1_send(1)
    pack(2)
    pack(3)
    arrived(rr.at[:, row], load_sem.at[1])
    split_right(row)
    s2_send(0)
    s3_send(0, 1, 2)
    s1_send(2)
    right_crossed(0, 4)
    s2_wait(0)
    s3_send(0, 3)
    s2_send(1)
    s4_send(0, 0)
    for d in (0, 1):
        right_second(d)
    s4_send(0, 1, 2)
    s3_send(1, 0)
    s2_send(2)
    s4_send(0, 3)
    s3_send(1, 1, 2)
    s2_wait(1)
    s3_send(1, 3)
    s1_send(3)
    s3_send(2, 0)
    for d in (0, 1):
        right_second_rest(d)
    for d in (0, 1):
        split_right(shard(-step[d]))
    for d in (0, 1):
        right_crossed(-step[d], 7 + d)
    s4_send(1, 0)
    s4_wait(0)
    collect(rl.at[0], a)

    def after(events, n):
        for step_, *given in events.get(n, ()):
            step_(*given)

    def after_by_core(events, n):
        if len(events) == 1 or events[0].get(n) == events[1].get(n):
            return after(events[0], n)
        for which in (0, 1):
            if n in events[which]:
                pl.when(core == which)(functools.partial(after, events[which], n))

    def multiply(start, *events):
        n = 0
        for u in range(0, CH, 256):
            src, dst = pl.ds(u, 256), pl.ds(start + u, 256)
            for out, times in ((out_h, times_hh), (out_l, times_ll), (out_c, times_cross)):
                out[dst, :] = times(a, b, src)
                after_by_core(events, n)
                n += 1

    def multiply_part(index, more, events):
        start = pl.multiple_of(index * 256, 256)
        n = 0
        for u in range(0, CH, 256):
            rows = pl.ds(u, 256)
            for out, terms in (
                (out_h, ((0, 1024),)),
                (out_l, ((1024, 0),)),
                (out_c, ((0, 0), (1024, 1024))),
            ):
                value = SCALE * sum(times_part(a, b, rows, start, *term) for term in terms)
                out[rows, :] = out[rows, :] + value if more else value
                after(events, n)
                n += 1

    multiply_part(x // 2, False, {1: ((right_third, 0), (right_third, 1))})
    s4_send(1, 1, 2)
    split_right(shard(2))
    right_crossed(2, 9)
    multiply_part(
        1 - x // 2,
        True,
        {
            1: ((s4_send, 1, 3), (s2_wait, 2), (s3_send, 2, 1, 2, 3)),
            3: ((s2_send, 3), (s3_send, 3, 0)),
        },
    )
    s4_wait(1)
    collect(rl.at[1], a)
    multiply(
        CH,
        {
            1: ((s4_send, 2, 0, 1),),
            2: ((s4_send, 2, 2, 3), (s3_send, 3, 1, 2)),
            3: ((s2_wait, 3), (s3_send, 3, 3)),
            5: ((s4_send, 3, 0),),
        },
        {2: ((s4_send, 2, 0, 1),), 3: ((s4_send, 2, 2, 3), (s2_wait, 3)), 4: ((s3_send, 3, 1),), 5: ((s3_send, 3, 2, 3),)},
    )
    s4_wait(2)
    collect(rl.at[2], a)
    multiply(
        2 * CH,
        {0: ((s4_send, 3, 1),), 1: ((s4_send, 3, 2),), 2: ((s4_send, 3, 3),)},
        {1: ((s4_send, 3, 0, 1),), 2: ((s4_send, 3, 2),), 3: ((s4_send, 3, 3),)},
    )
    s4_wait(3)
    arrived(rl.at[0, :, :, 0:3], near_sent.at[0])
    arrived(rl, far_sent.at[0])
    arrived(rr.at[:, 0:7], right_sent.at[0])


def finish_kernel(c_in, h_in, l_in, tiles, b, c_out, h_out, l_out, a, stage, sem):
    for i, (src, dst) in enumerate(((c_in, c_out), (h_in, h_out), (l_in, l_out))):
        for start in range(0, EARLY, CH):
            rows = pl.ds(start, CH)
            pltpu.make_async_copy(src.at[rows], dst.at[rows], sem.at[i]).start()
    collect(tiles, a)
    for u in range(2):
        rows = pl.ds(u * (LATE // 2), LATE // 2)
        for i, (times, dst) in enumerate(((times_cross, c_out), (times_hh, h_out), (times_ll, l_out))):
            stage[i, rows] = times(a, b, rows)
            here = pl.ds(EARLY + u * (LATE // 2), LATE // 2)
            pltpu.make_async_copy(stage.at[i, rows], dst.at[here], sem.at[i]).start()
    for i, dst in enumerate((c_out, h_out, l_out)):
        pltpu.make_async_copy(dst, dst, sem.at[i]).wait()


def per_device(left_h, left_l, right_h, right_l):
    dma = pltpu.SemaphoreType.DMA
    hbm, vmem = pl.BlockSpec(memory_space=pl.ANY), pl.BlockSpec(memory_space=pltpu.VMEM)
    early = pl.pallas_call(
        gather_kernel,
        out_shape=[pltpu.VMEM((EARLY, N), F32)] * 3
        + [pltpu.VMEM((2, 4, 4, SUB, 128), F32), pltpu.VMEM((4 * KW, N), BF16)],
        in_specs=[hbm] * 4,
        out_specs=[vmem] * 5,
        scratch_shapes=[
            pltpu.VMEM((2, KD, M), F32),
            pltpu.VMEM((NCH - 1, 2, 4, 4, SUB, 128), F32),
            pltpu.VMEM((2, 8, RD, N), F32),
            pltpu.VMEM((CH, 4 * KW), BF16),
            dma((2,)),
            dma((1,)), dma((1,)), dma((1,)), dma((NCH,)), dma((NCH,)), dma((NCH, 4)), dma((NCH,)), dma((10,)),
        ],
        compiler_params=pltpu.CompilerParams(
            collective_id=0, has_side_effects=True, vmem_limit_bytes=22 << 20
        ),
        cost_estimate=pl.CostEstimate(flops=24 * EARLY * N * KW, bytes_accessed=2 << 20, transcendentals=0),
        name="gather_multiply",
    )(*(pltpu.with_memory_space_constraint(v, pltpu.HBM) for v in (left_h.T, left_l.T, right_h, right_l)))
    return pl.pallas_call(
        finish_kernel,
        out_shape=[jax.ShapeDtypeStruct((M, N), F32)] * 3,
        in_specs=[vmem] * 5,
        out_specs=[hbm] * 3,
        scratch_shapes=[pltpu.VMEM((LATE, 4 * KW), BF16), pltpu.VMEM((3, LATE, N), F32), dma((3,))],
        compiler_params=pltpu.CompilerParams(vmem_limit_bytes=12 << 20),
        cost_estimate=pl.CostEstimate(flops=24 * LATE * N * KW, bytes_accessed=24 << 20, transcendentals=0),
        name="multiply_write",
    )(*(pltpu.with_memory_space_constraint(v, pltpu.VMEM) for v in early))


def solution(mesh):
    spec = P("row", "col")
    return jax.shard_map(
        per_device, mesh=mesh, in_specs=(spec,) * 4, out_specs=(spec,) * 3, check_vma=False
    )
```

```python
import functools

import jax
import jax.numpy as jnp
from jax import lax
from jax.experimental import pallas as pl
from jax.experimental.pallas import tpu as pltpu
from jax.sharding import PartitionSpec as P

KW = 512
SCALE = 2.0**30 / KW
MESH = pl.DeviceIdType.MESH
F32, BF16 = jnp.float32, jnp.bfloat16

M, N, KD, RD = 2048, 1024, 32, 64
CH = 512
NCH = M // CH
SUB = CH // 4
BLK = 16
LATE = CH
EARLY = M - LATE

dot = functools.partial(jnp.dot, preferred_element_type=F32)


def split(value):
    high = value.astype(BF16)
    return high, (value - high.astype(F32)).astype(BF16)


def times_hh(a, b, rows):
    return SCALE * (dot(a[rows, 0:1024], b[1024:2048, :]) + dot(a[rows, 512:1024], b[1024:1536, :]))


def times_ll(a, b, rows):
    return SCALE * (dot(a[rows, 1024:2048], b[0:1024, :]) + dot(a[rows, 1536:2048], b[0:512, :]))


def times_cross(a, b, rows):
    small = dot(a[rows, :], b[:, :])
    return SCALE * (small + (dot(a[rows, 512:1024], b[0:512, :]) + dot(a[rows, 1536:2048], b[1024:1536, :])))


def times_part(a, b, rows, start, left, right):
    low, high = a[rows, pl.ds(left + start, 256)], a[rows, pl.ds(left + 512 + start, 256)]
    b_high, b_low = b[pl.ds(right + start, 256), :], b[pl.ds(right + 512 + start, 256), :]
    return dot(low, b_high) + dot(high, b_low) + dot(high, b_high)


def collect(tiles, target):
    lane = lax.broadcasted_iota(jnp.int32, (BLK, 128), 1) // KD

    def body(g, carry):
        for arr in (0, 1):
            cols = pl.multiple_of(arr * 1024 + g * 128, 128)
            for r in range(0, SUB, BLK):
                source = [tiles[arr, g, q, pl.ds(r, BLK)] for q in range(4)]
                for j in range(4):
                    value = source[(3 - j) % 4]
                    for p in range(3):
                        value = jnp.where(lane == p, source[(p - j) % 4], value)
                    if j:
                        value = pltpu.roll(value, 128 - KD * j, 1)
                    high, low = split(value)
                    rows = pl.ds(j * SUB + r, BLK)
                    target[rows, pl.ds(cols, 128)] = low
                    target[rows, pl.ds(cols + 512, 128)] = high
        return carry

    lax.fori_loop(0, 4, body, 0)


def gather_kernel(
    lth, ltl, rth, rtl,
    out_c, out_h, out_l, rl_last, b,
    lt, rl, rr, a, load_sem,
    near_sent, far_sent, right_sent, s1r, s2r, s3r, s4r, rv,
):
    row, col = lax.axis_index("row"), lax.axis_index("col")
    x, core, y, z = row // 2, row % 2, col // 4, col % 4

    def wrap(v):
        return lax.rem(v + 8, 4)

    def at(dx=0, dc=0, dy=0, dz=0):
        new_core = 1 - core if dc else core
        return (wrap(x + dx) * 2 + new_core, wrap(y + dy) * 4 + wrap(z + dz))

    step = (1, -1)
    yz = tuple(tuple(at(dy=d) if ax == 0 else at(dz=d) for d in step) for ax in (0, 1))
    xs = tuple(at(dx=d) for d in step)
    twin = at(dc=1)

    barrier = pltpu.get_barrier_semaphore()
    for device in (*yz[0], *yz[1], *xs, twin):
        pl.semaphore_signal(barrier, 1, device_id=device, device_id_type=MESH)
    for i, ref in enumerate((lth, ltl)):
        pltpu.make_async_copy(ref, lt.at[i], load_sem.at[0]).start()
    for i, ref in enumerate((rth, rtl)):
        pltpu.make_async_copy(ref, rr.at[i, row], load_sem.at[1]).start()
    pltpu.make_async_copy(lt, lt, load_sem.at[0]).wait()

    def chunk(c):
        return rl_last if c == NCH - 1 else rl.at[c]

    def pack(c):
        for arr in (0, 1):
            parts = []
            for p in range(4):
                start = pl.multiple_of(c * CH + wrap(p - z) * SUB, SUB)
                parts.append(lt[arr, :, pl.ds(start, SUB)])
            chunk(c)[arr, y, z] = jnp.concatenate(parts, axis=0).T

    pack(0)
    pl.semaphore_wait(barrier, 7)

    def send(src, dst, send_sem, recv_sem, device):
        pltpu.make_async_remote_copy(
            src_ref=src, dst_ref=dst, send_sem=send_sem, recv_sem=recv_sem, device_id=device, device_id_type=MESH
        ).start()

    def arrived(ref, sem):
        pltpu.make_async_copy(ref, ref, sem).wait()

    off = (0, -1, 1, 2)
    both = [(d, arr) for d in (0, 1) for arr in (0, 1)]

    def tile(arr, first, second, c):
        f, s = wrap((y, z)[arr] + first), wrap((z, y)[arr] + second)
        return chunk(c).at[arr, f, s] if arr == 0 else chunk(c).at[arr, s, f]

    def half(ref, d):
        return ref.at[pl.ds(d * (SUB // 2), SUB // 2)]

    def s1_send(c):
        for d, arr in both:
            ref = tile(arr, 0, 0, c)
            send(ref, ref, near_sent.at[0], s1r.at[c], yz[arr][d])

    def s2_send(c):
        arrived(rl.at[0, 0, 0], s1r.at[c])
        for d, arr in both:
            ref = half(tile(arr, -step[d], 0, c), d)
            send(ref, ref, near_sent.at[0], s2r.at[c], yz[arr][d])

    def s2_wait(c):
        arrived(rl.at[0, 0, 0, 0:2], s2r.at[c])

    def s3_send(c, *ks):
        for k in ks:
            for d, arr in both:
                ref = tile(arr, off[k], 0, c)
                send(ref, ref, far_sent.at[0], s3r.at[c, k], yz[1 - arr][d])

    def s4_send(c, *ks):
        for k in ks:
            arrived(rl.at[0, 0, 0], s3r.at[c, k])
            for d, arr in both:
                ref = half(tile(arr, off[k], -step[d], c), d)
                send(ref, ref, far_sent.at[0], s4r.at[c], yz[1 - arr][d])

    def s4_wait(c):
        arrived(rl.at[0, 0, 0:2], s4r.at[c])

    def shard(dx, other=False):
        return wrap(x + dx) * 2 + (1 - core if other else core)

    def right_first():
        for arr, d in ((0, 0), (1, 1), (1, 0), (0, 1)):
            send((rth, rtl)[arr], rr.at[arr, row], right_sent.at[0], rv.at[arr * 2 + d], xs[d])
        for arr in (0, 1):
            send((rth, rtl)[arr], rr.at[arr, row], right_sent.at[0], rv.at[4], twin)

    def right_across(arr, dx, sem):
        ref = rr.at[arr, shard(dx)]
        send(ref, ref, right_sent.at[0], rv.at[sem], twin)

    def right_second(d):
        ref = rr.at[d, shard(-step[d])]
        arrived(ref, rv.at[d * 3])
        send(ref, ref, right_sent.at[0], rv.at[5 + d], xs[d])
        right_across(d, -step[d], 7 + d)

    def right_second_rest(d):
        arr = 1 - d
        arrived(rr.at[arr, shard(-step[d])], rv.at[arr * 2 + d])
        right_across(arr, -step[d], 7 + d)

    def right_third(d):
        arrived(rr.at[d, shard(2)], rv.at[5 + d])
        right_across(d, 2, 9)

    def right_crossed(dx, sem):
        arrived(rr.at[:, shard(dx, True)], rv.at[sem])
        split_right(shard(dx, True))

    def split_right(index):
        rows = pl.multiple_of(index * RD, RD)
        for arr, base in ((0, 1024), (1, 0)):
            high, low = split(rr[arr, index])
            b[pl.ds(base + rows, RD), :] = high
            b[pl.ds(base + 512 + rows, RD), :] = low

    s1_send(0)
    right_first()
    s3_send(0, 0)
    pack(1)
    s1_send(1)
    pack(2)
    pack(3)
    arrived(rr.at[:, row], load_sem.at[1])
    split_right(row)
    s2_send(0)
    s3_send(0, 1, 2)
    s1_send(2)
    right_crossed(0, 4)
    s2_wait(0)
    s3_send(0, 3)
    s2_send(1)
    s4_send(0, 0)
    for d in (0, 1):
        right_second(d)
    s4_send(0, 1, 2)
    s3_send(1, 0)
    s2_send(2)
    s4_send(0, 3)
    s3_send(1, 1, 2)
    s2_wait(1)
    s3_send(1, 3)
    s1_send(3)
    s3_send(2, 0)
    for d in (0, 1):
        right_second_rest(d)
    for d in (0, 1):
        split_right(shard(-step[d]))
    for d in (0, 1):
        right_crossed(-step[d], 7 + d)
    s4_send(1, 0)
    s4_wait(0)
    collect(rl.at[0], a)

    def after(events, n):
        for step_, *given in events.get(n, ()):
            step_(*given)

    def after_by_core(events, n):
        if len(events) == 1 or events[0].get(n) == events[1].get(n):
            return after(events[0], n)
        for which in (0, 1):
            if n in events[which]:
                pl.when(core == which)(functools.partial(after, events[which], n))

    def multiply(start, *events):
        n = 0
        for u in range(0, CH, 256):
            src, dst = pl.ds(u, 256), pl.ds(start + u, 256)
            for out, times in ((out_h, times_hh), (out_l, times_ll), (out_c, times_cross)):
                out[dst, :] = times(a, b, src)
                after_by_core(events, n)
                n += 1

    def multiply_part(index, more, events):
        start = pl.multiple_of(index * 256, 256)
        n = 0
        for u in range(0, CH, 256):
            rows = pl.ds(u, 256)
            for out, terms in (
                (out_h, ((0, 1024),)),
                (out_l, ((1024, 0),)),
                (out_c, ((0, 0), (1024, 1024))),
            ):
                value = SCALE * sum(times_part(a, b, rows, start, *term) for term in terms)
                out[rows, :] = out[rows, :] + value if more else value
                after(events, n)
                n += 1

    multiply_part(x // 2, False, {1: ((right_third, 0), (right_third, 1))})
    s4_send(1, 1, 2)
    split_right(shard(2))
    right_crossed(2, 9)
    multiply_part(
        1 - x // 2,
        True,
        {
            1: ((s4_send, 1, 3), (s2_wait, 2), (s3_send, 2, 1, 2, 3)),
            3: ((s2_send, 3), (s3_send, 3, 0)),
        },
    )
    s4_wait(1)
    collect(rl.at[1], a)
    multiply(
        CH,
        {
            1: ((s4_send, 2, 0, 1),),
            2: ((s4_send, 2, 2, 3), (s3_send, 3, 1, 2)),
            3: ((s2_wait, 3), (s3_send, 3, 3)),
            5: ((s4_send, 3, 0),),
        },
        {2: ((s4_send, 2, 0, 1),), 3: ((s4_send, 2, 2, 3), (s2_wait, 3)), 4: ((s3_send, 3, 1),), 5: ((s3_send, 3, 2, 3),)},
    )
    s4_wait(2)
    collect(rl.at[2], a)
    multiply(
        2 * CH,
        {0: ((s4_send, 3, 1),), 1: ((s4_send, 3, 2),), 2: ((s4_send, 3, 3),)},
        {1: ((s4_send, 3, 0, 1),), 2: ((s4_send, 3, 2),), 3: ((s4_send, 3, 3),)},
    )
    s4_wait(3)
    arrived(rl.at[0, :, :, 0:3], near_sent.at[0])
    arrived(rl, far_sent.at[0])
    arrived(rr.at[:, 0:7], right_sent.at[0])


def finish_kernel(c_in, h_in, l_in, tiles, b, c_out, h_out, l_out, a, stage, sem):
    for i, (src, dst) in enumerate(((c_in, c_out), (h_in, h_out), (l_in, l_out))):
        for start in range(0, EARLY, CH):
            rows = pl.ds(start, CH)
            pltpu.make_async_copy(src.at[rows], dst.at[rows], sem.at[i]).start()
    collect(tiles, a)
    for u in range(2):
        rows = pl.ds(u * (LATE // 2), LATE // 2)
        for i, (times, dst) in enumerate(((times_cross, c_out), (times_hh, h_out), (times_ll, l_out))):
            stage[i, rows] = times(a, b, rows)
            here = pl.ds(EARLY + u * (LATE // 2), LATE // 2)
            pltpu.make_async_copy(stage.at[i, rows], dst.at[here], sem.at[i]).start()
    for i, dst in enumerate((c_out, h_out, l_out)):
        pltpu.make_async_copy(dst, dst, sem.at[i]).wait()


def per_device(left_h, left_l, right_h, right_l):
    dma = pltpu.SemaphoreType.DMA
    hbm, vmem = pl.BlockSpec(memory_space=pl.ANY), pl.BlockSpec(memory_space=pltpu.VMEM)
    early = pl.pallas_call(
        gather_kernel,
        out_shape=[pltpu.VMEM((EARLY, N), F32)] * 3
        + [pltpu.VMEM((2, 4, 4, SUB, 128), F32), pltpu.VMEM((4 * KW, N), BF16)],
        in_specs=[hbm] * 4,
        out_specs=[vmem] * 5,
        scratch_shapes=[
            pltpu.VMEM((2, KD, M), F32),
            pltpu.VMEM((NCH - 1, 2, 4, 4, SUB, 128), F32),
            pltpu.VMEM((2, 8, RD, N), F32),
            pltpu.VMEM((CH, 4 * KW), BF16),
            dma((2,)),
            dma((1,)), dma((1,)), dma((1,)), dma((NCH,)), dma((NCH,)), dma((NCH, 4)), dma((NCH,)), dma((10,)),
        ],
        compiler_params=pltpu.CompilerParams(
            collective_id=0, has_side_effects=True, vmem_limit_bytes=22 << 20
        ),
        cost_estimate=pl.CostEstimate(flops=24 * EARLY * N * KW, bytes_accessed=2 << 20, transcendentals=0),
        name="gather_multiply",
    )(*(pltpu.with_memory_space_constraint(v, pltpu.HBM) for v in (left_h.T, left_l.T, right_h, right_l)))
    return pl.pallas_call(
        finish_kernel,
        out_shape=[jax.ShapeDtypeStruct((M, N), F32)] * 3,
        in_specs=[vmem] * 5,
        out_specs=[hbm] * 3,
        scratch_shapes=[pltpu.VMEM((LATE, 4 * KW), BF16), pltpu.VMEM((3, LATE, N), F32), dma((3,))],
        compiler_params=pltpu.CompilerParams(vmem_limit_bytes=12 << 20),
        cost_estimate=pl.CostEstimate(flops=24 * LATE * N * KW, bytes_accessed=24 << 20, transcendentals=0),
        name="multiply_write",
    )(*(pltpu.with_memory_space_constraint(v, pltpu.VMEM) for v in early))


def solution(mesh):
    spec = P("row", "col")
    return jax.shard_map(
        per_device, mesh=mesh, in_specs=(spec,) * 4, out_specs=(spec,) * 3, check_vma=False
    )
```
